256 devices in a mesh: samples: 32 (over x, z_lo, core), variants: 8 (over y, z_hi).
Axes of the slice: x: 4, y: 4, z: 8 (z_hi: 2, z_lo: 4; z = z_hi * 4 + z_lo), core: 2. Of those that a mesh axis runs over, the one named last changes fastest.
Arguments:
- dosage: bfloat16 [65536, 16384], P('samples', 'variants'), may hold values from 0 to 2, as said below
- sketch: bfloat16 [16384, 256], P(('variants', 'samples')), may hold values from -0.046875 to 0.046875
Outputs:
- basis: float32 [65536, 256], P(('samples', 'variants'))
- loadings: float32 [16384, 256], P(('variants', 'samples'))
The draws below stay inside these ranges and needn't reach their ends.
Inputs may be any that keep to these rules, and one draw needn't show every extreme that they name: `dosage`: imputed allele dosages.
All inputs are finite; a program needn't handle non-finite values.
Results may differ from the reference program's by a relative error of at most 0.0032.
Values may be sent and summed in bfloat16 or wider, within the bound.
A program may use at most 64 MiB of HBM per device.

```python
import math
import jax
import jax.numpy as jnp
from jax import lax

ROW_DEV = 2048
K = 256
NS = 65536
NV = 16384
N_SAMPLES = 32


def draw_dosage(key, part):
    key = jax.random.fold_in(key, 11)
    key_power, key_noise = jax.random.split(key, 2)
    power = jnp.exp(jax.random.uniform(key_power, (1, NV), jnp.float32, math.log(0.2), math.log(8.0)))
    level = 0.1 * 10.0 ** (jnp.arange(NS, dtype=jnp.float32) / max(NS - 1, 1))
    noise = jax.random.uniform(key_noise, (NS, NV), jnp.float32)
    base = noise ** power
    return (2.0 * level[:, None] * base).astype(jnp.bfloat16)


def block_scale(rng, extent, cuts, low, largest):
    def one(dim, blocks):
        draws = jax.random.uniform(jax.random.fold_in(jax.random.fold_in(rng, 6), dim), (blocks,), jnp.float32, low / len(cuts), largest / len(cuts))
        return jnp.repeat(jnp.exp(draws), extent[dim] // blocks).reshape((-1,) + (1,) * (len(extent) - dim - 1))

    factor_of = one(*cuts[0])
    for cut in cuts[1:]:
        factor_of = factor_of * one(*cut)
    return factor_of


def centred(key, shape, scale, limit, cuts=(), held_as=jnp.bfloat16):
    array = scale * jax.random.normal(key, shape, jnp.float32)
    if cuts:
        array = array * block_scale(key, shape, cuts, -0.22, 0.18)
    return jnp.clip(array, -limit, limit).astype(held_as)


def setup_inputs(seed: int = 0) -> dict:
    arg_keys = jax.random.split(jax.random.key(seed), 3)
    return {
        "dosage": draw_dosage(jax.random.fold_in(arg_keys[2], 71), 0),
        "sketch": centred(arg_keys[1], (NV, K), NV ** -0.5, 0.046875, ((0, 256),)),
    }


def reference(dosage, sketch):
    blocks = dosage.reshape(N_SAMPLES, ROW_DEV, NV)

    def add_total(carry, block):
        return (carry + lax.optimization_barrier(jnp.sum(block.astype(jnp.float32), axis=0)), None)
    total, unused = lax.scan(add_total, jnp.zeros((NV,), jnp.float32), blocks)
    mean = total / NS

    def add_spread(carry, block):
        centered = block.astype(jnp.float32) - mean
        return (carry + lax.optimization_barrier(jnp.sum(centered * centered, axis=0)), None)
    spread, unused = lax.scan(add_spread, jnp.zeros((NV,), jnp.float32), blocks)
    inv_sd = lax.rsqrt(spread / NS + 1e-05)
    weights = (inv_sd[:, None] * sketch.astype(jnp.float32)).astype(jnp.bfloat16)
    shift = jnp.dot(mean[None, :], weights.astype(jnp.float32), precision=lax.Precision.HIGHEST)

    def project(block):
        return jnp.dot(block.astype(jnp.float32), weights.astype(jnp.float32), preferred_element_type=jnp.float32) - shift
    projected = lax.map(project, blocks).reshape(NS, K)
    gram = jnp.dot(projected.T, projected, precision=lax.Precision.HIGHEST) / NS
    lower = jnp.linalg.cholesky(gram)
    basis = lax.linalg.triangular_solve(lower, projected, left_side=False, lower=True, transpose_a=True)
    basis_half = basis.astype(jnp.bfloat16)
    half_blocks = basis_half.reshape(N_SAMPLES, ROW_DEV, K)
    scale = inv_sd / math.sqrt(NS)

    def add_loading(carry, pair):
        block, piece = pair
        product = lax.dot_general(block.astype(jnp.float32), piece.astype(jnp.float32), (((0,), (0,)), ((), ())), preferred_element_type=jnp.float32)
        block_totals = lax.optimization_barrier(jnp.sum(piece.astype(jnp.float32), axis=0))
        partial_term = scale[:, None] * (product - mean[:, None] * block_totals[None, :])
        return (carry + partial_term, None)
    loadings, unused = lax.scan(add_loading, jnp.zeros((NV, K), jnp.float32), (blocks, half_blocks))
    return (basis, loadings)
```

```python
import functools
import math

import jax
import jax.numpy as jnp
from jax import lax
from jax.experimental import pallas as pl
from jax.experimental.pallas import tpu as pltpu
from jax.sharding import PartitionSpec as P

MESH = pl.DeviceIdType.MESH
HIGHEST = lax.Precision.HIGHEST
F32 = jnp.float32
BF16 = jnp.bfloat16
NX, NZL, NC, NY, NZH = 4, 4, 2, 4, 2
EPS = 1e-05


def coords():
    s = lax.axis_index("samples")
    v = lax.axis_index("variants")
    return s // 8, (s // 2) % 4, s % 2, v // 2, v % 2


def peer(dx=0, dzl=0, dc=0, dy=0, dzh=0):
    x, zl, c, y, zh = coords()
    x = (x + dx) % NX
    zl = (zl + dzl) % NZL
    c = (c + dc) % NC
    y = (y + dy) % NY
    zh = (zh + dzh) % NZH
    return ((x * NZL + zl) * NC + c, y * NZH + zh)


def loop(low, high, body):
    def step(k, carry):
        body(k)
        return carry

    lax.fori_loop(low, high, step, 0)


def comm_kernel(
    count, x_hbm, sk_ref, g_out, p_out, t_out,
    X, skbuf, W, st, st_c, st_x, st_z, Pp, yA, yB, zsend, zrecv,
    PG, TT, trecv, TM, tx, TX, tz, tfin, gbuf, grecv, gxy, gz, gfin,
    x_sem, c_ssem, c_rsem, sk_ssem, sk_rsem, st_ssem, st_rsem, y_ssem, y_rsem,
    z_ssem, z_rsem, g_ssem, g_rsem, t_ssem, t_rsem,
):
    x, zl, c, y, zh = coords()
    v = y * NZH + zh
    vz = y * NZH + (1 - zh)
    xz = x * NZL + zl
    xy = x * NY + y
    z = zh * NZL + zl
    blocks, rows, cols = X.shape
    local_count = blocks * rows

    def load(i):
        return pltpu.make_async_copy(x_hbm.at[pl.ds(i * rows, rows)], X.at[i], x_sem.at[i])

    def send(src, dst, ssem, rsem, to):
        return pltpu.make_async_remote_copy(
            src_ref=src, dst_ref=dst, send_sem=ssem, recv_sem=rsem, device_id=to, device_id_type=MESH
        )

    loop(0, blocks, lambda i: load(i).start())

    barrier = pltpu.get_barrier_semaphore()

    def greet(to):
        pl.semaphore_signal(barrier, inc=1, device_id=to, device_id_type=MESH)

    greet(peer(dc=1))
    loop(1, 16, lambda k: greet(peer(dx=k // 4, dzl=k % 4)))
    loop(0, 12, lambda k: greet(peer(dx=k // 3, dy=k % 3 + 1)))
    loop(0, 4, lambda k: greet(peer(dzl=k, dzh=1)))

    lane = 512
    pieces = cols // lane

    load(0).wait()
    pivots = []
    for h in range(pieces):

        def add_rows(r, acc, h=h):
            d = X[0, pl.ds(pl.multiple_of(r * 16, 16), 16), pl.ds(h * lane, lane)].astype(F32)
            return acc + (d[:8] + d[8:])

        acc = lax.fori_loop(0, rows // 16, add_rows, jnp.zeros((8, lane), F32), unroll=4)
        pivots.append(jnp.sum(acc, axis=0, keepdims=True) / rows)

    def spread_of(i, carry):
        out = []
        for h in range(pieces):

            def add_rows(r, acc, h=h):
                s1, s2 = acc
                d = X[i, pl.ds(pl.multiple_of(r * 16, 16), 16), pl.ds(h * lane, lane)].astype(F32) - pivots[h]
                q = d * d
                return s1 + (d[:8] + d[8:]), s2 + (q[:8] + q[8:])

            out.append(lax.fori_loop(0, rows // 16, add_rows, carry[h], unroll=4))
        return tuple(out)

    zero = jnp.zeros((8, lane), F32)
    sums = tuple((zero, zero) for _ in range(pieces))
    half = blocks // 2

    def block_sums(i, carry):
        @pl.when(i > 0)
        def _():
            load(i).wait()

        return spread_of(i, carry)

    sums = lax.fori_loop(0, half, block_sums, sums)

    pl.semaphore_wait(barrier, 32)

    def sketch_copy(k):
        return send(sk_ref, skbuf.at[xz, c], sk_ssem.at[k], sk_rsem.at[k], peer(dx=k // 4, dzl=k % 4))

    loop(1, 16, lambda k: sketch_copy(k).start())
    skbuf[xz, c] = sk_ref[...]

    sums = lax.fori_loop(half, blocks, block_sums, sums)

    for h in range(pieces):
        s1 = jnp.sum(sums[h][0], axis=0, keepdims=True)
        s2 = jnp.sum(sums[h][1], axis=0, keepdims=True)
        mean = pivots[h] + s1 / local_count
        m2 = s2 - s1 * s1 / local_count
        for q in range(lane // 128):
            g = h * (lane // 128) + q
            st[g : g + 1, :] = mean[:, q * 128 : (q + 1) * 128]
            st[16 + g : 17 + g, :] = m2[:, q * 128 : (q + 1) * 128]

    copy = send(st, st_c, c_ssem.at[0], c_rsem.at[0], peer(dc=1))
    copy.start()
    copy.wait()
    a, b = st[...], st_c[...]
    n = float(local_count)
    delta = a[:16] - b[:16]
    st_x[x, :16] = 0.5 * (a[:16] + b[:16])
    st_x[x, 16:] = a[16:] + b[16:] + (0.5 * n) * delta * delta
    n = 2.0 * n

    def merge(ref, n):
        mean = 0.25 * ((ref[0, :16] + ref[1, :16]) + (ref[2, :16] + ref[3, :16]))
        m2 = (ref[0, 16:] + ref[1, 16:]) + (ref[2, 16:] + ref[3, 16:])
        for i in range(4):
            d = ref[i, :16] - mean
            m2 = m2 + n * (d * d)
        return mean, m2

    def stat_x(k):
        return send(st_x.at[x], st_x.at[x], st_ssem.at[k], st_rsem.at[k], peer(dx=k))

    def stat_z(k):
        return send(st_z.at[zl], st_z.at[zl], st_ssem.at[4 + k], st_rsem.at[4 + k], peer(dzl=k))

    loop(1, 4, lambda k: stat_x(k).start())
    loop(1, 4, lambda k: stat_x(k).wait())
    mean, m2 = merge(st_x, n)
    n = 4.0 * n
    st_z[zl, :16] = mean
    st_z[zl, 16:] = m2
    loop(1, 4, lambda k: stat_z(k).start())

    loop(1, 16, lambda k: sketch_copy(k).wait())
    sketch_core = send(skbuf.at[:, c], skbuf.at[:, c], c_ssem.at[1], c_rsem.at[1], peer(dc=1))
    sketch_core.start()

    loop(1, 4, lambda k: stat_z(k).wait())
    mean, m2 = merge(st_z, n)
    inv_sd = lax.rsqrt(m2 / count + EPS)
    st[:16, :] = mean
    st[16:, :] = inv_sd
    columns = jnp.transpose(jnp.concatenate([mean, inv_sd, jnp.zeros((96, 128), F32)], axis=0))
    sketch_core.wait()

    shift = jnp.zeros((8, 256), F32)
    for g in range(16):
        sk = skbuf[g].reshape(128, 256).astype(F32)
        w = (columns[:, 16 + g : 17 + g] * sk).astype(BF16)
        W[g * 128 : (g + 1) * 128, :] = w
        shift = shift + jnp.sum((columns[:, g : g + 1] * w.astype(F32)).reshape(16, 8, 256), axis=0)
    shift = jnp.sum(shift, axis=0, keepdims=True)

    def project(i):
        Pp[i] = jnp.dot(X[i], W[...], preferred_element_type=F32) - shift

    def copy_a(k):
        return send(Pp.at[((y + k) % NY) * NZH + (1 - zh)], yA.at[y], y_ssem.at[k], y_rsem.at[k], peer(dy=k))

    def copy_b(k):
        return send(Pp.at[((y + k) % NY) * NZH + zh], yB.at[y], y_ssem.at[4 + k], y_rsem.at[4 + k], peer(dy=k))

    def project_a(k):
        project(((y + k) % NY) * NZH + (1 - zh))

        @pl.when(k < 4)
        def _():
            copy_a(k).start()

    def project_b(k):
        project(((y + k) % NY) * NZH + zh)

    loop(1, 5, project_a)
    loop(1, 5, project_b)

    loop(1, 4, lambda k: copy_a(k).wait())
    zsend[...] = (Pp[vz] + yA[(y + 1) % NY]) + (yA[(y + 2) % NY] + yA[(y + 3) % NY])
    z_copy = send(zsend, zrecv, z_ssem.at[0], z_rsem.at[0], peer(dzh=1))
    z_copy.start()
    loop(1, 4, lambda k: copy_b(k).start())
    loop(1, 4, lambda k: copy_b(k).wait())
    own = (Pp[v] + yB[(y + 1) % NY]) + (yB[(y + 2) % NY] + yB[(y + 3) % NY])
    z_copy.wait()
    own = own + zrecv[...]
    p_out[...] = own

    PG[v] = jnp.transpose(own).astype(BF16)

    def gather_own(k):
        return send(PG.at[v], PG.at[v], y_ssem.at[8 + k], y_rsem.at[8 + k], peer(dy=k))

    def gather_other(k):
        return send(PG.at[vz], PG.at[vz], y_ssem.at[12 + k], y_rsem.at[12 + k], peer(dy=k))

    gather_z = send(PG.at[v], PG.at[v], z_ssem.at[1], z_rsem.at[1], peer(dzh=1))
    gather_z.start()
    loop(1, 4, lambda k: gather_own(k).start())

    gram = lax.dot_general(own, own, (((0,), (0,)), ((), ())), precision=HIGHEST, preferred_element_type=F32)
    gbuf[...] = (gram / count).reshape(gbuf.shape)
    g_core = send(gbuf.at[1 - c], grecv, c_ssem.at[2], c_rsem.at[2], peer(dc=1))
    g_core.start()
    g_core.wait()
    gbuf[c] = gbuf[c] + grecv[...]
    gxy[xy] = gbuf[c, xy]

    def gram_scatter(k):
        to = ((x + k // 4) % NX) * NY + (y + k % 4) % NY
        return send(gbuf.at[c, to], gxy.at[xy], g_ssem.at[k], g_rsem.at[k], peer(dx=k // 4, dy=k % 4))

    def gram_z(k):
        return send(gz.at[z], gz.at[z], g_ssem.at[16 + k], g_rsem.at[16 + k], peer(dzh=k // 4, dzl=k % 4))

    def gram_gather(k):
        return send(gfin.at[c, xy], gfin.at[c, xy], g_ssem.at[24 + k], g_rsem.at[24 + k], peer(dx=k // 4, dy=k % 4))

    loop(1, 16, lambda k: gram_scatter(k).start())
    loop(1, 16, lambda k: gram_scatter(k).wait())
    gz[z] = jnp.sum(gxy[...], axis=0)
    loop(1, 8, lambda k: gram_z(k).start())

    gather_z.wait()
    loop(1, 4, lambda k: gather_other(k).start())

    loop(1, 8, lambda k: gram_z(k).wait())
    gfin[c, xy] = jnp.sum(gz[...], axis=0)
    loop(1, 16, lambda k: gram_gather(k).start())

    loop(1, 4, lambda k: gather_own(k).wait())

    def first_product(j):
        at = pl.ds(pl.multiple_of(j * 256, 256), 256)
        acc = jnp.zeros((256, 256), F32)
        for q in range(NY):
            i = q * NZH + zh
            acc = acc + jnp.dot(PG[i], X[i, :, at], preferred_element_type=F32)
        TT[:, at] = acc

    loop(0, cols // 256, first_product)

    loop(1, 16, lambda k: gram_gather(k).wait())
    g_back = send(gfin.at[c], gfin.at[c], c_ssem.at[3], c_rsem.at[3], peer(dc=1))
    g_back.start()

    loop(1, 4, lambda k: gather_other(k).wait())
    total = jnp.zeros((256, 128), F32)
    for i in range(8):
        part = PG[i].astype(F32)
        total = total + (part[:, :128] + part[:, 128:])
    total = jnp.sum(total, axis=1, keepdims=True)
    root = math.sqrt(count)

    def second_product(j):
        at = pl.ds(pl.multiple_of(j * 256, 256), 256)
        acc = TT[:, at]
        for q in range(NY):
            i = q * NZH + (1 - zh)
            acc = acc + jnp.dot(PG[i], X[i, :, at], preferred_element_type=F32)
        for q in range(2):
            g = 2 * j + q
            part = acc[:, q * 128 : (q + 1) * 128]
            part = (st[pl.ds(16 + g, 1), :] / root) * (part - total * st[pl.ds(g, 1), :])
            TT[:, pl.ds(pl.multiple_of(g * 128, 128), 128)] = part

    loop(0, cols // 256, second_product)
    g_back.wait()
    g_out[...] = gfin[...].reshape(256, 256)

    t_core = send(TT.at[pl.ds(pl.multiple_of((1 - c) * 128, 128), 128)], trecv, c_ssem.at[4], c_rsem.at[4], peer(dc=1))
    t_core.start()
    t_core.wait()
    mine = pl.ds(pl.multiple_of(c * 128, 128), 128)

    def merge_core(j):
        at = pl.ds(pl.multiple_of(j * 512, 512), 512)
        TM[j] = TT[mine, at] + trecv[:, at]

    loop(0, 4, merge_core)

    def t_x(k):
        return send(TM.at[(x + k) % NX], tx.at[x], t_ssem.at[k], t_rsem.at[k], peer(dx=k))

    def t_z(k):
        return send(TX.at[(zl + k) % NZL], tz.at[zl], t_ssem.at[4 + k], t_rsem.at[4 + k], peer(dzl=k))

    loop(1, 4, lambda k: t_x(k).start())
    loop(1, 4, lambda k: t_x(k).wait())
    acc = (TM[x] + tx[(x + 1) % NX]) + (tx[(x + 2) % NX] + tx[(x + 3) % NX])
    for q in range(NZL):
        TX[q] = acc[:, q * 128 : (q + 1) * 128]
    loop(1, 4, lambda k: t_z(k).start())
    loop(1, 4, lambda k: t_z(k).wait())
    tfin[mine] = (TX[zl] + tz[(zl + 1) % NZL]) + (tz[(zl + 2) % NZL] + tz[(zl + 3) % NZL])
    t_back = send(tfin.at[mine], tfin.at[mine], c_ssem.at[5], c_rsem.at[5], peer(dc=1))
    t_back.start()
    t_back.wait()
    t_out[...] = tfin[...]


def communicate(dosage, sketch, count):
    rows, cols = dosage.shape
    k = sketch.shape[1]
    vm = pltpu.VMEM
    dma = pltpu.SemaphoreType.DMA
    vmem = pl.BlockSpec(memory_space=pltpu.VMEM)
    return pl.pallas_call(
        functools.partial(comm_kernel, count),
        out_shape=(
            jax.ShapeDtypeStruct((k, k), F32),
            jax.ShapeDtypeStruct((rows // 8, k), F32),
            jax.ShapeDtypeStruct((k, 128), F32),
        ),
        in_specs=[pl.BlockSpec(memory_space=pl.ANY), vmem],
        out_specs=(vmem, vmem, vmem),
        scratch_shapes=[
            vm((8, rows // 8, cols), BF16),
            vm((16, 2, 64, k), BF16),
            vm((cols, k), BF16),
            vm((32, 128), F32),
            vm((32, 128), F32),
            vm((4, 32, 128), F32),
            vm((4, 32, 128), F32),
            vm((8, rows // 8, k), F32),
            vm((4, rows // 8, k), F32),
            vm((4, rows // 8, k), F32),
            vm((rows // 8, k), F32),
            vm((rows // 8, k), F32),
            vm((8, k, rows // 8), BF16),
            vm((k, cols), F32),
            vm((k // 2, cols), F32),
            vm((4, k // 2, cols // 4), F32),
            vm((4, k // 2, cols // 4), F32),
            vm((4, k // 2, 128), F32),
            vm((4, k // 2, 128), F32),
            vm((k, 128), F32),
            vm((2, 16, 8, k), F32),
            vm((16, 8, k), F32),
            vm((16, 8, k), F32),
            vm((8, 8, k), F32),
            vm((2, 16, 8, k), F32),
            dma((8,)),
            dma((6,)), dma((6,)),
            dma((16,)), dma((16,)),
            dma((8,)), dma((8,)),
            dma((16,)), dma((16,)),
            dma((2,)), dma((2,)),
            dma((40,)), dma((40,)),
            dma((8,)), dma((8,)),
        ],
        compiler_params=pltpu.CompilerParams(
            collective_id=0, has_side_effects=True, vmem_limit_bytes=56 * 2**20
        ),
        name="power_step",
    )(dosage, sketch)


NB = 64


def factor_kernel(g_ref, p_ref, t_ref, basis_ref, load_ref, M, Y):
    n = g_ref.shape[0]
    M[:, :n] = g_ref[...]
    row = lax.broadcasted_iota(jnp.int32, (n, n), 0)
    col = lax.broadcasted_iota(jnp.int32, (n, n), 1)
    M[:, n:] = (row == col).astype(F32)
    eye = (lax.broadcasted_iota(jnp.int32, (NB, NB), 0) == lax.broadcasted_iota(jnp.int32, (NB, NB), 1)).astype(F32)
    for b in range(n // NB):
        at = slice(b * NB, (b + 1) * NB)
        D = jnp.concatenate([M[at, at], eye], axis=1)
        for i in range(NB):
            r = lax.rsqrt(D[i : i + 1, i : i + 1])
            y = D[i : i + 1, :] * r
            Y[i : i + 1, :] = y
            if i + 1 < NB:
                D = D - (D[:, i : i + 1] * r) * y
        panel = jnp.dot(Y[:, NB:], M[at, :], precision=HIGHEST, preferred_element_type=F32)
        M[at, :] = panel
        if (b + 1) * NB < n:
            rest = slice((b + 1) * NB, n)
            M[rest, :] = M[rest, :] - lax.dot_general(
                panel[:, rest], panel, (((0,), (0,)), ((), ())), precision=HIGHEST, preferred_element_type=F32
            )
    inverse = M[:, n:]
    basis_ref[...] = lax.dot_general(
        p_ref[...], inverse, (((1,), (1,)), ((), ())), precision=HIGHEST, preferred_element_type=F32
    )
    loads = jnp.transpose(jnp.dot(inverse, t_ref[...], precision=HIGHEST, preferred_element_type=F32))
    c = lax.axis_index("samples") % NC
    load_ref[...] = jnp.where(c == 0, loads[:64], loads[64:])


def finish(gram, projected, t):
    n = gram.shape[0]
    vmem = pl.BlockSpec(memory_space=pltpu.VMEM)
    return pl.pallas_call(
        factor_kernel,
        out_shape=(
            jax.ShapeDtypeStruct(projected.shape, F32),
            jax.ShapeDtypeStruct((64, n), F32),
        ),
        in_specs=[vmem, vmem, vmem],
        out_specs=(vmem, vmem),
        scratch_shapes=[pltpu.VMEM((n, 2 * n), F32), pltpu.VMEM((NB, 2 * NB), F32)],
        compiler_params=pltpu.CompilerParams(vmem_limit_bytes=32 * 2**20),
        name="factor",
    )(gram, projected, t)


def local(dosage, sketch):
    count = dosage.shape[0] * lax.axis_size("samples")
    gram, projected, t = communicate(dosage, sketch, count)
    return finish(gram, projected, t)


def solution(mesh):
    in_specs = (P("samples", "variants"), P(("variants", "samples"), None))
    out_specs = (P(("samples", "variants"), None), P(("variants", "samples"), None))
    return jax.shard_map(local, mesh=mesh, in_specs=in_specs, out_specs=out_specs, check_vma=False)
```

```python
import functools
import math

import jax
import jax.numpy as jnp
from jax import lax
from jax.experimental import pallas as pl
from jax.experimental.pallas import tpu as pltpu
from jax.sharding import PartitionSpec as P

MESH = pl.DeviceIdType.MESH
HIGHEST = lax.Precision.HIGHEST
F32 = jnp.float32
BF16 = jnp.bfloat16
NX, NZL, NC, NY, NZH = 4, 4, 2, 4, 2
EPS = 1e-05


def coords():
    s = lax.axis_index("samples")
    v = lax.axis_index("variants")
    return s // 8, (s // 2) % 4, s % 2, v // 2, v % 2


def peer(dx=0, dzl=0, dc=0, dy=0, dzh=0):
    x, zl, c, y, zh = coords()
    x = (x + dx) % NX
    zl = (zl + dzl) % NZL
    c = (c + dc) % NC
    y = (y + dy) % NY
    zh = (zh + dzh) % NZH
    return ((x * NZL + zl) * NC + c, y * NZH + zh)


def loop(low, high, body):
    def step(k, carry):
        body(k)
        return carry

    lax.fori_loop(low, high, step, 0)


def iota(shape, axis):
    return lax.broadcasted_iota(jnp.int32, shape, axis)


NB = 64


def factor_diagonal(D, Y):
    big = (8, 128)
    n8 = NB // 8
    D = [D[8 * m : 8 * m + 8, :] for m in range(n8)]
    sub = iota(big, 0)
    for q in range(n8):
        rows = [jnp.broadcast_to(D[q][i : i + 1, :], big) for i in range(8)]
        lanes = [[jnp.broadcast_to(D[m][:, 8 * q + c : 8 * q + c + 1], big) for c in range(8)] for m in range(q, n8)]
        a = [[jnp.broadcast_to(lanes[0][c][i : i + 1, :], big) if c <= i else None for c in range(8)] for i in range(8)]
        r, l, y, z = [None] * 8, [[None] * 8 for _ in range(8)], [None] * 8, [None] * 8
        for i in range(8):
            r[i] = lax.rsqrt(a[i][i])
            for k in range(i + 1, 8):
                l[k][i] = a[k][i] * r[i]
            for k in range(i + 1, 8):
                for c in range(i + 1, k + 1):
                    a[k][c] = a[k][c] - l[k][i] * l[c][i]
            y[i] = rows[i] * r[i]
            for k in range(i + 1, 8):
                rows[k] = rows[k] - l[k][i] * y[i]
        out = y[0]
        for i in range(1, 8):
            out = jnp.where(sub == i, y[i], out)
        Y[8 * q : 8 * q + 8, :] = out
        for i in range(7, -1, -1):
            acc = y[i]
            for k in range(i + 1, 8):
                acc = acc - l[k][i] * z[k]
            z[i] = acc * r[i]
        for m in range(q + 1, n8):
            s = [lanes[m - q][k] * z[k] for k in range(8)]
            D[m] = D[m] - (((s[0] + s[1]) + (s[2] + s[3])) + ((s[4] + s[5]) + (s[6] + s[7])))


def factor_rows(M, Y, b):
    n = M.shape[0]
    at = slice(b * NB, (b + 1) * NB)
    eye = (iota((NB, NB), 0) == iota((NB, NB), 1)).astype(F32)
    factor_diagonal(jnp.concatenate([M[at, at], eye], axis=1), Y)
    panel = jnp.dot(Y[:, NB:], M[at, :], precision=HIGHEST, preferred_element_type=F32)
    M[at, :] = panel
    if (b + 1) * NB < n:
        rest = slice((b + 1) * NB, n)
        M[rest, :] = M[rest, :] - lax.dot_general(
            panel[:, rest], panel, (((0,), (0,)), ((), ())), precision=HIGHEST, preferred_element_type=F32
        )


def comm_kernel(
    count, x_hbm, sk_ref, basis_ref, load_ref,
    X, skbuf, W, st, st_c, st_x, st_z, Pp, tr, di, mg, zsend, zrecv,
    PG, TT, trecv, TM, tx, TX, tz, tfin, gbuf, grecv, gxy, gz, gfin, M, Y, own_rows,
    x_sem, c_ssem, c_rsem, sk_ssem, sk_rsem, fw_ssem, fw_rsem, st_ssem, st_rsem, y_ssem, y_rsem,
    z_ssem, z_rsem, g_ssem, g_rsem, t_ssem, t_rsem, tc_ssem, tc_rsem,
):
    x, zl, c, y, zh = coords()
    v = y * NZH + zh
    vz = y * NZH + (1 - zh)
    xz = x * NZL + zl
    xy = x * NY + y
    z = zh * NZL + zl
    blocks, rows, cols = X.shape
    local_count = blocks * rows

    def load(i):
        return pltpu.make_async_copy(x_hbm.at[pl.ds(i * rows, rows)], X.at[i], x_sem.at[i])

    def send(src, dst, ssem, rsem, to):
        return pltpu.make_async_remote_copy(
            src_ref=src, dst_ref=dst, send_sem=ssem, recv_sem=rsem, device_id=to, device_id_type=MESH
        )

    barrier = pltpu.get_barrier_semaphore()

    def greet(to):
        pl.semaphore_signal(barrier, inc=1, device_id=to, device_id_type=MESH)

    loop(0, 4, lambda k: greet(peer(dzl=k, dzh=1)))
    loop(0, 9, lambda k: greet(peer(dx=k // 3 + 1, dy=k % 3 + 1)))
    loop(0, blocks, lambda i: load(i).start())
    loop(1, 4, lambda k: greet(peer(dzl=k)))
    loop(1, 4, lambda k: greet(peer(dx=k)))
    loop(1, 4, lambda k: greet(peer(dy=k)))
    greet(peer(dc=1))

    lane = 512
    order = (1, 3, 2)
    pieces = cols // lane

    load(0).wait()
    pivots = []
    for h in range(pieces):

        def add_rows(r, acc, h=h):
            d = X[0, pl.ds(pl.multiple_of(r * 16, 16), 16), pl.ds(h * lane, lane)].astype(F32)
            return acc + (d[:8] + d[8:])

        acc = lax.fori_loop(0, rows // 16, add_rows, jnp.zeros((8, lane), F32), unroll=4)
        pivots.append(jnp.sum(acc, axis=0, keepdims=True) / rows)

    def spread_of(i, carry):
        out = []
        for h in range(pieces):

            def add_rows(r, acc, h=h):
                s1, s2 = acc
                d = X[i, pl.ds(pl.multiple_of(r * 16, 16), 16), pl.ds(h * lane, lane)].astype(F32) - pivots[h]
                q = d * d
                return s1 + (d[:8] + d[8:]), s2 + (q[:8] + q[8:])

            out.append(lax.fori_loop(0, rows // 16, add_rows, carry[h], unroll=4))
        return tuple(out)

    zero = jnp.zeros((8, lane), F32)
    sums = tuple((zero, zero) for _ in range(pieces))
    def block_sums(i, carry):
        @pl.when(i > 0)
        def _():
            load(i).wait()

        return spread_of(i, carry)

    early = 3
    sums = lax.fori_loop(0, early, block_sums, sums)

    pl.semaphore_wait(barrier, 23)

    def sketch_x(k):
        return send(sk_ref, skbuf.at[xz, c], sk_ssem.at[k], sk_rsem.at[k], peer(dx=k))

    def sketch_z(k):
        return send(sk_ref, skbuf.at[xz, c], sk_ssem.at[4 + k], sk_rsem.at[4 + k], peer(dzl=k))

    def sketch_zx(j, k):
        at = x * NZL + (zl + NZL - j) % NZL
        i = 4 * j + 4 + k
        return send(skbuf.at[at, c], skbuf.at[at, c], sk_ssem.at[i], sk_rsem.at[i], peer(dx=k))

    def sketch_core(k):
        at = pl.ds(((x + k) % NX) * NZL, NZL)
        return send(skbuf.at[at, c], skbuf.at[at, c], fw_ssem.at[k], fw_rsem.at[k], peer(dc=1))

    for k in order:
        sketch_z(k).start()
    for k in order:
        sketch_x(k).start()
    skbuf[xz, c] = sk_ref[...]

    sums = lax.fori_loop(early, blocks, block_sums, sums)

    for h in range(pieces):
        s1 = jnp.sum(sums[h][0], axis=0, keepdims=True)
        s2 = jnp.sum(sums[h][1], axis=0, keepdims=True)
        mean = pivots[h] + s1 / local_count
        m2 = s2 - s1 * s1 / local_count
        for q in range(lane // 128):
            g = h * (lane // 128) + q
            st[g : g + 1, :] = mean[:, q * 128 : (q + 1) * 128]
            st[16 + g : 17 + g, :] = m2[:, q * 128 : (q + 1) * 128]

    copy = send(st, st_c, c_ssem.at[0], c_rsem.at[0], peer(dc=1))
    copy.start()
    copy.wait()
    a, b = st[...], st_c[...]
    n = float(local_count)
    delta = a[:16] - b[:16]
    st_x[x, :16] = 0.5 * (a[:16] + b[:16])
    st_x[x, 16:] = a[16:] + b[16:] + (0.5 * n) * delta * delta
    n = 2.0 * n

    def merge(ref, n):
        mean = 0.25 * ((ref[0, :16] + ref[1, :16]) + (ref[2, :16] + ref[3, :16]))
        m2 = (ref[0, 16:] + ref[1, 16:]) + (ref[2, 16:] + ref[3, 16:])
        for i in range(4):
            d = ref[i, :16] - mean
            m2 = m2 + n * (d * d)
        return mean, m2

    def stat_x(k):
        return send(st_x.at[x], st_x.at[x], st_ssem.at[k], st_rsem.at[k], peer(dx=k))

    def stat_z(k):
        return send(st_z.at[zl], st_z.at[zl], st_ssem.at[4 + k], st_rsem.at[4 + k], peer(dzl=k))

    for k in order:
        stat_x(k).start()
    for j in order:
        sketch_z(j).wait()
        for k in order:
            sketch_zx(j, k).start()
    sketch_core(0).start()

    for k in order:
        stat_x(k).wait()
    mean, m2 = merge(st_x, n)
    n = 4.0 * n
    st_z[zl, :16] = mean
    st_z[zl, 16:] = m2
    loop(1, 4, lambda k: stat_z(k).start())

    loop(1, 4, lambda k: stat_z(k).wait())
    mean, m2 = merge(st_z, n)
    inv_sd = lax.rsqrt(m2 / count + EPS)
    st[:16, :] = mean
    st[16:, :] = inv_sd
    columns = jnp.transpose(jnp.concatenate([mean, inv_sd, jnp.zeros((96, 128), F32)], axis=0))

    for k in order:
        sketch_x(k).wait()
        for j in order:
            sketch_zx(j, k).wait()
        sketch_core(4 - k).start()
    for k in range(NX):
        sketch_core(k).wait()

    shift = jnp.zeros((8, 256), F32)
    for g in range(16):
        sk = skbuf[g].reshape(128, 256).astype(F32)
        w = (columns[:, 16 + g : 17 + g] * sk).astype(BF16)
        W[g * 128 : (g + 1) * 128, :] = w
        shift = shift + jnp.sum((columns[:, g : g + 1] * w.astype(F32)).reshape(16, 8, 256), axis=0)
    shift = jnp.sum(shift, axis=0, keepdims=True)

    def project(i):
        Pp[i] = jnp.dot(X[i], W[...], preferred_element_type=F32) - shift

    size = rows // 2
    half = size // 2

    def block(dy, p):
        return ((y + dy) % NY) * NZH + (1 - zh if p < 2 else zh)

    def part(dy, p, h):
        return Pp.at[block(dy, p), pl.ds(p % 2 * size + h * half, half)]

    def transit(p, h):
        i = 6 * p + h
        return send(part(2, p, h), tr.at[p, h], y_ssem.at[i], y_rsem.at[i], peer(dy=1 if h == 0 else 3))

    def direct(p, h):
        i = 6 * p + 2 + h
        dy = 3 if h == 0 else 1
        return send(part(dy, p, h), di.at[p, h], y_ssem.at[i], y_rsem.at[i], peer(dy=dy))

    def merged(p, h):
        i = 6 * p + 4 + h
        dy = 1 if h == 0 else 3
        return send(part(dy, p, h), mg.at[p, h], y_ssem.at[i], y_rsem.at[i], peer(dy=dy))

    def start(copy, p):
        copy(p, 0).start()
        copy(p, 1).start()

    def pass_on(p):
        for h in range(2):
            transit(p, h).wait()
            at = pl.ds(p % 2 * size + h * half, half)
            i = block(1 if h == 0 else 3, p)
            Pp[i, at] = Pp[i, at] + tr[p, h]
            merged(p, h).start()

    def arrived(p):
        for h in range(2):
            direct(p, h).wait()
            merged(p, h).wait()
        return Pp[block(0, p), pl.ds(p % 2 * size, size)] + (di[p] + mg[p]).reshape(size, -1)

    def z_copy(p):
        return send(zsend.at[p], zrecv.at[p], z_ssem.at[p], z_rsem.at[p], peer(dzh=1))

    project(block(2, 0))
    start(transit, 0)
    start(transit, 1)
    project(block(1, 0))
    project(block(3, 0))
    start(direct, 0)
    start(direct, 1)
    for i in (block(0, 0), block(2, 2), block(1, 2), block(3, 2), block(0, 2)):
        project(i)
    pass_on(0)
    pass_on(1)
    zsend[0] = arrived(0)
    z_copy(0).start()
    start(transit, 2)
    zsend[1] = arrived(1)
    z_copy(1).start()
    start(transit, 3)
    start(direct, 2)
    start(direct, 3)
    pass_on(2)
    pass_on(3)
    for p in range(2):
        here = arrived(2 + p)
        z_copy(p).wait()
        own_rows[p * size : (p + 1) * size] = here + zrecv[p]
    own = own_rows[...]

    PG[v] = jnp.transpose(own).astype(BF16)

    def gather_own(k):
        return send(PG.at[v], PG.at[v], y_ssem.at[24 + k], y_rsem.at[24 + k], peer(dy=k))

    def gather_other(k):
        return send(PG.at[vz], PG.at[vz], y_ssem.at[28 + k], y_rsem.at[28 + k], peer(dy=k))

    gather_z = send(PG.at[v], PG.at[v], z_ssem.at[2], z_rsem.at[2], peer(dzh=1))
    gather_z.start()

    gram = lax.dot_general(own, own, (((0,), (0,)), ((), ())), precision=HIGHEST, preferred_element_type=F32)
    gbuf[...] = (gram / count).reshape(gbuf.shape)
    g_core = send(gbuf.at[1 - c], grecv, c_ssem.at[2], c_rsem.at[2], peer(dc=1))
    g_core.start()
    for k in order:
        gather_own(k).start()
    g_core.wait()
    gbuf[c] = gbuf[c] + grecv[...]
    gxy[xy] = gbuf[c, xy]

    def gram_scatter(k):
        to = ((x + k // 4) % NX) * NY + (y + k % 4) % NY
        return send(gbuf.at[c, to], gxy.at[xy], g_ssem.at[k], g_rsem.at[k], peer(dx=k // 4, dy=k % 4))

    def gram_z(k):
        return send(gz.at[z], gz.at[z], g_ssem.at[16 + k], g_rsem.at[16 + k], peer(dzh=k // 4, dzl=k % 4))

    def gram_gather(k):
        return send(gfin.at[c, xy], gfin.at[c, xy], g_ssem.at[24 + k], g_rsem.at[24 + k], peer(dx=k // 4, dy=k % 4))

    loop(1, 16, lambda k: gram_scatter(k).start())
    loop(1, 16, lambda k: gram_scatter(k).wait())
    gz[z] = jnp.sum(gxy[...], axis=0)
    loop(1, 8, lambda k: gram_z(k).start())
    gather_z.wait()
    for k in order:
        gather_other(k).start()


    loop(1, 8, lambda k: gram_z(k).wait())
    gfin[c, xy] = jnp.sum(gz[...], axis=0)
    loop(1, 16, lambda k: gram_gather(k).start())

    loop(1, 4, lambda k: gather_own(k).wait())

    def products(j, which):
        at = pl.ds(pl.multiple_of(j * 256, 256), 256)
        acc = jnp.zeros((256, 256), F32)
        for i in which:
            acc = acc + jnp.dot(PG[i], X[i, :, at], preferred_element_type=F32)
        return acc.reshape(2, 128, 256)

    def first_product(j):
        TT[j] = products(j, [q * NZH + zh for q in range(NY)] + [vz])

    loop(0, 8, first_product)

    loop(1, 4, lambda k: gather_other(k).wait())
    total = jnp.zeros((256, 128), F32)
    for i in range(8):
        part = PG[i].astype(F32)
        total = total + (part[:, :128] + part[:, 128:])
    total = jnp.sum(total, axis=1, keepdims=True).reshape(2, 128, 1)
    root = math.sqrt(count)

    def t_core(j):
        return send(TT.at[j, 1 - c], trecv.at[j], tc_ssem.at[j], tc_rsem.at[j], peer(dc=1))

    def second_product(j):
        acc = TT[j] + products(j, [((y + k) % NY) * NZH + 1 - zh for k in order])
        mean = jnp.concatenate([st[pl.ds(2 * j, 1), :], st[pl.ds(2 * j + 1, 1), :]], axis=1)
        inv_sd = jnp.concatenate([st[pl.ds(16 + 2 * j, 1), :], st[pl.ds(17 + 2 * j, 1), :]], axis=1)
        TT[j] = (inv_sd / root) * (acc - total * mean)
        t_core(j).start()

    for k in order + (0,):
        first = ((x + k) % NX) * 2
        loop(0, 2, lambda q: second_product(first + q))

    def t_x(k, h):
        to = ((x + k) % NX) * 2
        at = pl.ds(h * 64, 64)
        i = 4 * h + k
        return send(TM.at[pl.ds(to, 2), at], tx.at[x, :, at], t_ssem.at[i], t_rsem.at[i], peer(dx=k))

    def t_z(k, h):
        i = 8 + 4 * h + k
        return send(TX.at[h, (zl + k) % NZL], tz.at[h, zl], t_ssem.at[i], t_rsem.at[i], peer(dzl=k))

    def merge_x(h):
        for k in order:
            t_x(k, h).wait()
        at = pl.ds(h * 64, 64)
        acc = TM[pl.ds(2 * x, 2), at]
        for k in order:
            acc = acc + tx[(x + k) % NX, :, at]
        for q in range(NZL):
            TX[h, q] = acc[q // 2, :, q % 2 * 128 : q % 2 * 128 + 128]
        for k in order:
            t_z(k, h).start()

    for k in order + (0,):
        for q in range(2):
            j = ((x + k) % NX) * 2 + q
            t_core(j).wait()
            TM[j] = TT[j, c] + trecv[j]
        if k:
            t_x(k, 0).start()
    for k in order:
        t_x(k, 1).start()

    loop(1, 16, lambda k: gram_gather(k).wait())
    g_back = send(gfin.at[c], gfin.at[c], c_ssem.at[3], c_rsem.at[3], peer(dc=1))
    g_back.start()
    g_back.wait()
    n = own.shape[1]
    M[:, :n] = gfin[...].reshape(n, n)
    M[:, n:] = (iota((n, n), 0) == iota((n, n), 1)).astype(F32)

    factor_rows(M, Y, 0)
    merge_x(0)
    factor_rows(M, Y, 1)
    factor_rows(M, Y, 2)
    merge_x(1)
    factor_rows(M, Y, 3)
    basis_ref[...] = lax.dot_general(
        own_rows[...], M[:, n:], (((1,), (1,)), ((), ())), precision=HIGHEST, preferred_element_type=F32
    )
    mine = pl.ds(pl.multiple_of(c * 128, 128), 128)
    for h in range(2):
        for k in order:
            t_z(k, h).wait()
        acc = TX[h, zl]
        for k in order:
            acc = acc + tz[h, (zl + k) % NZL]
        tfin[pl.ds(pl.multiple_of(c * 128 + h * 64, 64), 64)] = acc
    t_back = send(tfin.at[mine], tfin.at[mine], c_ssem.at[5], c_rsem.at[5], peer(dc=1))
    t_back.start()
    t_back.wait()
    loads = jnp.transpose(jnp.dot(M[:, n:], tfin[...], precision=HIGHEST, preferred_element_type=F32))
    load_ref[...] = jnp.where(c == 0, loads[:64], loads[64:])


def power_step(dosage, sketch, count):
    rows, cols = dosage.shape
    k = sketch.shape[1]
    vm = pltpu.VMEM
    dma = pltpu.SemaphoreType.DMA
    vmem = pl.BlockSpec(memory_space=pltpu.VMEM)
    return pl.pallas_call(
        functools.partial(comm_kernel, count),
        out_shape=(
            jax.ShapeDtypeStruct((rows // 8, k), F32),
            jax.ShapeDtypeStruct((64, k), F32),
        ),
        in_specs=[pl.BlockSpec(memory_space=pl.ANY), vmem],
        out_specs=(vmem, vmem),
        scratch_shapes=[
            vm((8, rows // 8, cols), BF16),
            vm((16, 2, 64, k), BF16),
            vm((cols, k), BF16),
            vm((32, 128), F32),
            vm((32, 128), F32),
            vm((4, 32, 128), F32),
            vm((4, 32, 128), F32),
            vm((8, rows // 8, k), F32),
            vm((4, 2, rows // 32, k), F32),
            vm((4, 2, rows // 32, k), F32),
            vm((4, 2, rows // 32, k), F32),
            vm((2, rows // 16, k), F32),
            vm((2, rows // 16, k), F32),
            vm((8, k, rows // 8), BF16),
            vm((8, 2, k // 2, cols // 8), F32),
            vm((8, k // 2, cols // 8), F32),
            vm((8, k // 2, cols // 8), F32),
            vm((4, 2, k // 2, cols // 8), F32),
            vm((2, 4, k // 4, 128), F32),
            vm((2, 4, k // 4, 128), F32),
            vm((k, 128), F32),
            vm((2, 16, 8, k), F32),
            vm((16, 8, k), F32),
            vm((16, 8, k), F32),
            vm((8, 8, k), F32),
            vm((2, 16, 8, k), F32),
            vm((k, 2 * k), F32),
            vm((NB, 2 * NB), F32),
            vm((rows // 8, k), F32),
            dma((8,)),
            dma((6,)), dma((6,)),
            dma((20,)), dma((20,)),
            dma((4,)), dma((4,)),
            dma((8,)), dma((8,)),
            dma((32,)), dma((32,)),
            dma((3,)), dma((3,)),
            dma((40,)), dma((40,)),
            dma((16,)), dma((16,)),
            dma((8,)), dma((8,)),
        ],
        compiler_params=pltpu.CompilerParams(
            collective_id=0, has_side_effects=True, vmem_limit_bytes=56 * 2**20
        ),
        name="power_step",
    )(dosage, sketch)


def local(dosage, sketch):
    count = dosage.shape[0] * lax.axis_size("samples")
    return power_step(dosage, sketch, count)


def solution(mesh):
    in_specs = (P("samples", "variants"), P(("variants", "samples"), None))
    out_specs = (P(("samples", "variants"), None), P(("variants", "samples"), None))
    return jax.shard_map(local, mesh=mesh, in_specs=in_specs, out_specs=out_specs, check_vma=False)
```

```python
import functools
import math

import jax
import jax.numpy as jnp
from jax import lax
from jax.experimental import pallas as pl
from jax.experimental.pallas import tpu as pltpu
from jax.sharding import PartitionSpec as P

MESH = pl.DeviceIdType.MESH
HIGHEST = lax.Precision.HIGHEST
F32 = jnp.float32
BF16 = jnp.bfloat16
NX, NZL, NC, NY, NZH = 4, 4, 2, 4, 2
EPS = 1e-05


def coords():
    s = lax.axis_index("samples")
    v = lax.axis_index("variants")
    return s // 8, (s // 2) % 4, s % 2, v // 2, v % 2


def peer(dx=0, dzl=0, dc=0, dy=0, dzh=0):
    x, zl, c, y, zh = coords()
    x = (x + dx) % NX
    zl = (zl + dzl) % NZL
    c = (c + dc) % NC
    y = (y + dy) % NY
    zh = (zh + dzh) % NZH
    return ((x * NZL + zl) * NC + c, y * NZH + zh)


def loop(low, high, body):
    def step(k, carry):
        body(k)
        return carry

    lax.fori_loop(low, high, step, 0)


def iota(shape, axis):
    return lax.broadcasted_iota(jnp.int32, shape, axis)


NB = 64


def factor_diagonal(D, Y):
    big = (8, 128)
    n8 = NB // 8
    D = [D[8 * m : 8 * m + 8, :] for m in range(n8)]
    sub = iota(big, 0)
    for q in range(n8):
        rows = [jnp.broadcast_to(D[q][i : i + 1, :], big) for i in range(8)]
        lanes = [[jnp.broadcast_to(D[m][:, 8 * q + c : 8 * q + c + 1], big) for c in range(8)] for m in range(q, n8)]
        a = [[jnp.broadcast_to(lanes[0][c][i : i + 1, :], big) if c <= i else None for c in range(8)] for i in range(8)]
        r, l, y, z = [None] * 8, [[None] * 8 for _ in range(8)], [None] * 8, [None] * 8
        for i in range(8):
            r[i] = lax.rsqrt(a[i][i])
            for k in range(i + 1, 8):
                l[k][i] = a[k][i] * r[i]
            for k in range(i + 1, 8):
                for c in range(i + 1, k + 1):
                    a[k][c] = a[k][c] - l[k][i] * l[c][i]
            y[i] = rows[i] * r[i]
            for k in range(i + 1, 8):
                rows[k] = rows[k] - l[k][i] * y[i]
        out = y[0]
        for i in range(1, 8):
            out = jnp.where(sub == i, y[i], out)
        Y[8 * q : 8 * q + 8, :] = out
        for i in range(7, -1, -1):
            acc = y[i]
            for k in range(i + 1, 8):
                acc = acc - l[k][i] * z[k]
            z[i] = acc * r[i]
        for m in range(q + 1, n8):
            s = [lanes[m - q][k] * z[k] for k in range(8)]
            D[m] = D[m] - (((s[0] + s[1]) + (s[2] + s[3])) + ((s[4] + s[5]) + (s[6] + s[7])))


def factor_rows(M, Y, b):
    n = M.shape[0]
    at = slice(b * NB, (b + 1) * NB)
    eye = (iota((NB, NB), 0) == iota((NB, NB), 1)).astype(F32)
    factor_diagonal(jnp.concatenate([M[at, at], eye], axis=1), Y)
    first = b * NB // 128 * 128
    last = n + -(-(b + 1) * NB // 128) * 128
    panel = jnp.dot(Y[:, NB:], M[at, first:last], precision=HIGHEST, preferred_element_type=F32)
    M[at, first:last] = panel
    if (b + 1) * NB < n:
        rest = slice((b + 1) * NB, n)
        M[rest, first:last] = M[rest, first:last] - lax.dot_general(
            panel[:, (b + 1) * NB - first : n - first],
            panel,
            (((0,), (0,)), ((), ())),
            precision=HIGHEST,
            preferred_element_type=F32,
        )


def comm_kernel(
    count, x_hbm, sk_ref, basis_ref, load_ref,
    X, skbuf, W, st, st_c, st_x, st_z, Pp, tr, di, mg, zsend, zrecv,
    PG, TT, trecv, TM, tx, TX, tz, tfin, gbuf, grecv, gxy, gz, gfin, M, Y, own_rows,
    x_sem, c_ssem, c_rsem, sk_ssem, sk_rsem, fw_ssem, fw_rsem, st_ssem, st_rsem, y_ssem, y_rsem,
    z_ssem, z_rsem, g_ssem, g_rsem, t_ssem, t_rsem, tc_ssem, tc_rsem,
):
    x, zl, c, y, zh = coords()
    v = y * NZH + zh
    vz = y * NZH + (1 - zh)
    xz = x * NZL + zl
    xy = x * NY + y
    z = zh * NZL + zl
    blocks, rows, cols = X.shape
    local_count = blocks * rows

    def load(i):
        return pltpu.make_async_copy(x_hbm.at[pl.ds(i * rows, rows)], X.at[i], x_sem.at[i])

    def send(src, dst, ssem, rsem, to):
        return pltpu.make_async_remote_copy(
            src_ref=src, dst_ref=dst, send_sem=ssem, recv_sem=rsem, device_id=to, device_id_type=MESH
        )

    barrier = pltpu.get_barrier_semaphore()

    def greet(to):
        pl.semaphore_signal(barrier, inc=1, device_id=to, device_id_type=MESH)

    loop(0, 4, lambda k: greet(peer(dzl=k, dzh=1)))
    loop(0, 9, lambda k: greet(peer(dx=k // 3 + 1, dy=k % 3 + 1)))
    loop(0, blocks, lambda i: load(i).start())
    loop(1, 4, lambda k: greet(peer(dzl=k)))
    loop(1, 4, lambda k: greet(peer(dx=k)))
    loop(1, 4, lambda k: greet(peer(dy=k)))
    greet(peer(dc=1))

    lane = 512
    order = (1, 3, 2)
    pieces = cols // lane

    load(0).wait()
    pivots = []
    for h in range(pieces):

        def add_rows(r, acc, h=h):
            d = X[0, pl.ds(pl.multiple_of(r * 16, 16), 16), pl.ds(h * lane, lane)].astype(F32)
            return acc + (d[:8] + d[8:])

        acc = lax.fori_loop(0, rows // 16, add_rows, jnp.zeros((8, lane), F32), unroll=4)
        pivots.append(jnp.sum(acc, axis=0, keepdims=True) / rows)

    def spread_of(i, carry):
        out = []
        for h in range(pieces):

            def add_rows(r, acc, h=h):
                s1, s2 = acc
                d = X[i, pl.ds(pl.multiple_of(r * 16, 16), 16), pl.ds(h * lane, lane)].astype(F32) - pivots[h]
                q = d * d
                return s1 + (d[:8] + d[8:]), s2 + (q[:8] + q[8:])

            out.append(lax.fori_loop(0, rows // 16, add_rows, carry[h], unroll=4))
        return tuple(out)

    zero = jnp.zeros((8, lane), F32)
    sums = tuple((zero, zero) for _ in range(pieces))
    def block_sums(i, carry):
        @pl.when(i > 0)
        def _():
            load(i).wait()

        return spread_of(i, carry)

    early = 3
    sums = lax.fori_loop(0, early, block_sums, sums)

    pl.semaphore_wait(barrier, 23)

    def sketch_x(k):
        return send(sk_ref, skbuf.at[xz, c], sk_ssem.at[k], sk_rsem.at[k], peer(dx=k))

    def sketch_z(k):
        return send(sk_ref, skbuf.at[xz, c], sk_ssem.at[4 + k], sk_rsem.at[4 + k], peer(dzl=k))

    def sketch_zx(j, k):
        at = x * NZL + (zl + NZL - j) % NZL
        i = 4 * j + 4 + k
        return send(skbuf.at[at, c], skbuf.at[at, c], sk_ssem.at[i], sk_rsem.at[i], peer(dx=k))

    def sketch_core(k):
        at = pl.ds(((x + k) % NX) * NZL, NZL)
        return send(skbuf.at[at, c], skbuf.at[at, c], fw_ssem.at[k], fw_rsem.at[k], peer(dc=1))

    for k in order:
        sketch_z(k).start()
    for k in order:
        sketch_x(k).start()
    skbuf[xz, c] = sk_ref[...]

    sums = lax.fori_loop(early, blocks, block_sums, sums)

    for h in range(pieces):
        s1 = jnp.sum(sums[h][0], axis=0, keepdims=True)
        s2 = jnp.sum(sums[h][1], axis=0, keepdims=True)
        mean = pivots[h] + s1 / local_count
        m2 = s2 - s1 * s1 / local_count
        for q in range(lane // 128):
            g = h * (lane // 128) + q
            st[g : g + 1, :] = mean[:, q * 128 : (q + 1) * 128]
            st[16 + g : 17 + g, :] = m2[:, q * 128 : (q + 1) * 128]

    copy = send(st, st_c, c_ssem.at[0], c_rsem.at[0], peer(dc=1))
    copy.start()
    copy.wait()
    a, b = st[...], st_c[...]
    n = float(local_count)
    delta = a[:16] - b[:16]
    st_x[x, :16] = 0.5 * (a[:16] + b[:16])
    st_x[x, 16:] = a[16:] + b[16:] + (0.5 * n) * delta * delta
    n = 2.0 * n

    def merge(ref, n):
        mean = 0.25 * ((ref[0, :16] + ref[1, :16]) + (ref[2, :16] + ref[3, :16]))
        m2 = (ref[0, 16:] + ref[1, 16:]) + (ref[2, 16:] + ref[3, 16:])
        for i in range(4):
            d = ref[i, :16] - mean
            m2 = m2 + n * (d * d)
        return mean, m2

    def stat_x(k):
        return send(st_x.at[x], st_x.at[x], st_ssem.at[k], st_rsem.at[k], peer(dx=k))

    def stat_z(k):
        return send(st_z.at[zl], st_z.at[zl], st_ssem.at[4 + k], st_rsem.at[4 + k], peer(dzl=k))

    for k in order:
        stat_x(k).start()
    for j in order:
        sketch_z(j).wait()
        for k in order:
            sketch_zx(j, k).start()
    sketch_core(0).start()

    for k in order:
        stat_x(k).wait()
    mean, m2 = merge(st_x, n)
    n = 4.0 * n
    st_z[zl, :16] = mean
    st_z[zl, 16:] = m2
    loop(1, 4, lambda k: stat_z(k).start())

    loop(1, 4, lambda k: stat_z(k).wait())
    mean, m2 = merge(st_z, n)
    inv_sd = lax.rsqrt(m2 / count + EPS)
    st[:16, :] = mean
    st[16:, :] = inv_sd
    columns = jnp.transpose(jnp.concatenate([mean, inv_sd, jnp.zeros((96, 128), F32)], axis=0))

    for k in order:
        sketch_x(k).wait()
        for j in order:
            sketch_zx(j, k).wait()
        sketch_core(4 - k).start()
    for k in range(NX):
        sketch_core(k).wait()

    shift = jnp.zeros((8, 256), F32)
    for g in range(16):
        sk = skbuf[g].reshape(128, 256).astype(F32)
        w = (columns[:, 16 + g : 17 + g] * sk).astype(BF16)
        W[g * 128 : (g + 1) * 128, :] = w
        shift = shift + jnp.sum((columns[:, g : g + 1] * w.astype(F32)).reshape(16, 8, 256), axis=0)
    shift = jnp.sum(shift, axis=0, keepdims=True)

    def project(i):
        Pp[i] = jnp.dot(X[i], W[...], preferred_element_type=F32) - shift

    size = rows // 2
    half = size // 2

    def block(dy, p):
        return ((y + dy) % NY) * NZH + (1 - zh if p < 2 else zh)

    def part(dy, p, h):
        return Pp.at[block(dy, p), pl.ds(p % 2 * size + h * half, half)]

    def transit(p, h):
        i = 6 * p + h
        return send(part(2, p, h), tr.at[p, h], y_ssem.at[i], y_rsem.at[i], peer(dy=1 if h == 0 else 3))

    def direct(p, h):
        i = 6 * p + 2 + h
        dy = 3 if h == 0 else 1
        return send(part(dy, p, h), di.at[p, h], y_ssem.at[i], y_rsem.at[i], peer(dy=dy))

    def merged(p, h):
        i = 6 * p + 4 + h
        dy = 1 if h == 0 else 3
        return send(part(dy, p, h), mg.at[p, h], y_ssem.at[i], y_rsem.at[i], peer(dy=dy))

    def start(copy, p):
        copy(p, 0).start()
        copy(p, 1).start()

    def pass_on(p):
        for h in range(2):
            transit(p, h).wait()
            at = pl.ds(p % 2 * size + h * half, half)
            i = block(1 if h == 0 else 3, p)
            Pp[i, at] = Pp[i, at] + tr[p, h]
            merged(p, h).start()

    def arrived(p):
        for h in range(2):
            direct(p, h).wait()
            merged(p, h).wait()
        return Pp[block(0, p), pl.ds(p % 2 * size, size)] + (di[p] + mg[p]).reshape(size, -1)

    def z_copy(p):
        return send(zsend.at[p], zrecv.at[p], z_ssem.at[p], z_rsem.at[p], peer(dzh=1))

    project(block(2, 0))
    start(transit, 0)
    start(transit, 1)
    loop(0, 2, lambda q: project(block(1 + 2 * q, 0)))
    start(direct, 0)
    start(direct, 1)
    loop(0, 5, lambda q: project(((y + q) % NY) * NZH + zh + (4 - q) // 4 * (1 - 2 * zh)))
    pass_on(0)
    pass_on(1)
    zsend[0] = arrived(0)
    z_copy(0).start()
    start(transit, 2)
    zsend[1] = arrived(1)
    z_copy(1).start()
    start(transit, 3)
    start(direct, 2)
    start(direct, 3)
    pass_on(2)
    pass_on(3)
    for p in range(2):
        here = arrived(2 + p)
        z_copy(p).wait()
        own_rows[p * size : (p + 1) * size] = here + zrecv[p]
    own = own_rows[...]

    PG[v] = jnp.transpose(own).astype(BF16)

    def gather_own(k):
        return send(PG.at[v], PG.at[v], y_ssem.at[24 + k], y_rsem.at[24 + k], peer(dy=k))

    def gather_other(k):
        return send(PG.at[vz], PG.at[vz], y_ssem.at[28 + k], y_rsem.at[28 + k], peer(dy=k))

    gather_z = send(PG.at[v], PG.at[v], z_ssem.at[2], z_rsem.at[2], peer(dzh=1))
    gather_z.start()

    gram = lax.dot_general(own, own, (((0,), (0,)), ((), ())), precision=HIGHEST, preferred_element_type=F32)
    gbuf[...] = (gram / count).reshape(gbuf.shape)
    g_core = send(gbuf.at[1 - c], grecv, c_ssem.at[2], c_rsem.at[2], peer(dc=1))
    g_core.start()
    g_core.wait()
    gbuf[c] = gbuf[c] + grecv[...]
    gxy[xy] = gbuf[c, xy]

    def gram_scatter(k):
        to = ((x + k // 4) % NX) * NY + (y + k % 4) % NY
        return send(gbuf.at[c, to], gxy.at[xy], g_ssem.at[k], g_rsem.at[k], peer(dx=k // 4, dy=k % 4))

    def gram_z(k):
        return send(gz.at[z], gz.at[z], g_ssem.at[16 + k], g_rsem.at[16 + k], peer(dzh=k // 4, dzl=k % 4))

    def gram_gather(k):
        return send(gfin.at[c, xy], gfin.at[c, xy], g_ssem.at[24 + k], g_rsem.at[24 + k], peer(dx=k // 4, dy=k % 4))

    loop(1, 16, lambda k: gram_scatter(k).start())
    for k in order:
        gather_own(k).start()
    gather_z.wait()
    for k in order:
        gather_other(k).start()
    loop(1, 16, lambda k: gram_scatter(k).wait())
    gz[z] = jnp.sum(gxy[...], axis=0)
    loop(1, 8, lambda k: gram_z(k).start())


    loop(1, 8, lambda k: gram_z(k).wait())
    gfin[c, xy] = jnp.sum(gz[...], axis=0)
    loop(1, 16, lambda k: gram_gather(k).start())

    loop(1, 4, lambda k: gather_own(k).wait())

    def products(j, which):
        at = pl.ds(pl.multiple_of(j * 256, 256), 256)
        acc = jnp.zeros((256, 256), F32)
        for i in which:
            acc = acc + jnp.dot(PG[i], X[i, :, at], preferred_element_type=F32)
        return acc.reshape(2, 128, 256)

    def first_product(j):
        TT[j] = products(j, [q * NZH + zh for q in range(NY)] + [vz])

    loop(0, 8, first_product)

    loop(1, 4, lambda k: gather_other(k).wait())
    total = jnp.zeros((256, 128), F32)
    for i in range(8):
        part = PG[i].astype(F32)
        total = total + (part[:, :128] + part[:, 128:])
    total = jnp.sum(total, axis=1, keepdims=True).reshape(2, 128, 1)
    root = math.sqrt(count)

    def t_core(j):
        return send(TT.at[j, 1 - c], trecv.at[j], tc_ssem.at[j], tc_rsem.at[j], peer(dc=1))

    def second_product(j):
        acc = TT[j] + products(j, [((y + k) % NY) * NZH + 1 - zh for k in order])
        mean = jnp.concatenate([st[pl.ds(2 * j, 1), :], st[pl.ds(2 * j + 1, 1), :]], axis=1)
        inv_sd = jnp.concatenate([st[pl.ds(16 + 2 * j, 1), :], st[pl.ds(17 + 2 * j, 1), :]], axis=1)
        TT[j] = (inv_sd / root) * (acc - total * mean)
        t_core(j).start()

    for k in order + (0,):
        first = ((x + k) % NX) * 2
        loop(0, 2, lambda q: second_product(first + q))

    def t_x(k, h):
        to = ((x + k) % NX) * 2
        at = pl.ds(h * 64, 64)
        i = 4 * h + k
        return send(TM.at[pl.ds(to, 2), at], tx.at[x, :, at], t_ssem.at[i], t_rsem.at[i], peer(dx=k))

    def t_z(k, h):
        i = 8 + 4 * h + k
        return send(TX.at[h, (zl + k) % NZL], tz.at[h, zl], t_ssem.at[i], t_rsem.at[i], peer(dzl=k))

    def merge_x(h):
        for k in order:
            t_x(k, h).wait()
        at = pl.ds(h * 64, 64)
        acc = TM[pl.ds(2 * x, 2), at]
        for k in order:
            acc = acc + tx[(x + k) % NX, :, at]
        for q in range(NZL):
            TX[h, q] = acc[q // 2, :, q % 2 * 128 : q % 2 * 128 + 128]
        for k in order:
            t_z(k, h).start()

    for k in order + (0,):
        for q in range(2):
            j = ((x + k) % NX) * 2 + q
            t_core(j).wait()
            TM[j] = TT[j, c] + trecv[j]
        if k:
            t_x(k, 0).start()
    for k in order:
        t_x(k, 1).start()

    loop(1, 16, lambda k: gram_gather(k).wait())
    g_back = send(gfin.at[c], gfin.at[c], c_ssem.at[3], c_rsem.at[3], peer(dc=1))
    g_back.start()
    g_back.wait()
    n = own.shape[1]
    M[:, :n] = gfin[...].reshape(n, n)
    M[:, n:] = (iota((n, n), 0) == iota((n, n), 1)).astype(F32)

    factor_rows(M, Y, 0)
    factor_rows(M, Y, 1)
    merge_x(0)
    factor_rows(M, Y, 2)
    merge_x(1)
    factor_rows(M, Y, 3)
    basis_ref[...] = lax.dot_general(
        own_rows[...], M[:, n:], (((1,), (1,)), ((), ())), precision=HIGHEST, preferred_element_type=F32
    )
    mine = pl.ds(pl.multiple_of(c * 128, 128), 128)
    for h in range(2):
        for k in order:
            t_z(k, h).wait()
        acc = TX[h, zl]
        for k in order:
            acc = acc + tz[h, (zl + k) % NZL]
        tfin[pl.ds(pl.multiple_of(c * 128 + h * 64, 64), 64)] = acc
    t_back = send(tfin.at[mine], tfin.at[mine], c_ssem.at[5], c_rsem.at[5], peer(dc=1))
    t_back.start()
    t_back.wait()
    loads = jnp.transpose(jnp.dot(M[:, n:], tfin[...], precision=HIGHEST, preferred_element_type=F32))
    load_ref[...] = jnp.where(c == 0, loads[:64], loads[64:])


def power_step(dosage, sketch, count):
    rows, cols = dosage.shape
    k = sketch.shape[1]
    vm = pltpu.VMEM
    dma = pltpu.SemaphoreType.DMA
    vmem = pl.BlockSpec(memory_space=pltpu.VMEM)
    return pl.pallas_call(
        functools.partial(comm_kernel, count),
        out_shape=(
            pltpu.VMEM((rows // 8, k), F32),
            pltpu.VMEM((64, k), F32),
        ),
        in_specs=[pl.BlockSpec(memory_space=pl.ANY), vmem],
        out_specs=(vmem, vmem),
        scratch_shapes=[
            vm((8, rows // 8, cols), BF16),
            vm((16, 2, 64, k), BF16),
            vm((cols, k), BF16),
            vm((32, 128), F32),
            vm((32, 128), F32),
            vm((4, 32, 128), F32),
            vm((4, 32, 128), F32),
            vm((8, rows // 8, k), F32),
            vm((4, 2, rows // 32, k), F32),
            vm((4, 2, rows // 32, k), F32),
            vm((4, 2, rows // 32, k), F32),
            vm((2, rows // 16, k), F32),
            vm((2, rows // 16, k), F32),
            vm((8, k, rows // 8), BF16),
            vm((8, 2, k // 2, cols // 8), F32),
            vm((8, k // 2, cols // 8), F32),
            vm((8, k // 2, cols // 8), F32),
            vm((4, 2, k // 2, cols // 8), F32),
            vm((2, 4, k // 4, 128), F32),
            vm((2, 4, k // 4, 128), F32),
            vm((k, 128), F32),
            vm((2, 16, 8, k), F32),
            vm((16, 8, k), F32),
            vm((16, 8, k), F32),
            vm((8, 8, k), F32),
            vm((2, 16, 8, k), F32),
            vm((k, 2 * k), F32),
            vm((NB, 2 * NB), F32),
            vm((rows // 8, k), F32),
            dma((8,)),
            dma((6,)), dma((6,)),
            dma((20,)), dma((20,)),
            dma((4,)), dma((4,)),
            dma((8,)), dma((8,)),
            dma((32,)), dma((32,)),
            dma((3,)), dma((3,)),
            dma((40,)), dma((40,)),
            dma((16,)), dma((16,)),
            dma((8,)), dma((8,)),
        ],
        compiler_params=pltpu.CompilerParams(
            collective_id=0, has_side_effects=True, vmem_limit_bytes=56 * 2**20
        ),
        name="power_step",
    )(dosage, sketch)


def store_kernel(basis_ref, load_ref, basis_out, load_out, sem):
    copies = [
        pltpu.make_async_copy(basis_ref, basis_out, sem.at[0]),
        pltpu.make_async_copy(load_ref, load_out, sem.at[1]),
    ]
    for copy in copies:
        copy.start()
    for copy in copies:
        copy.wait()


def store(basis, loadings):
    vmem = pl.BlockSpec(memory_space=pltpu.VMEM)
    hbm = pl.BlockSpec(memory_space=pltpu.HBM)
    return pl.pallas_call(
        store_kernel,
        out_shape=(jax.ShapeDtypeStruct(basis.shape, F32), jax.ShapeDtypeStruct(loadings.shape, F32)),
        in_specs=[vmem, vmem],
        out_specs=(hbm, hbm),
        scratch_shapes=[pltpu.SemaphoreType.DMA((2,))],
        name="store",
    )(basis, loadings)


def local(dosage, sketch):
    count = dosage.shape[0] * lax.axis_size("samples")
    return store(*power_step(dosage, sketch, count))


def solution(mesh):
    in_specs = (P("samples", "variants"), P(("variants", "samples"), None))
    out_specs = (P(("samples", "variants"), None), P(("variants", "samples"), None))
    return jax.shard_map(local, mesh=mesh, in_specs=in_specs, out_specs=out_specs, check_vma=False)
```

```python
import functools
import math

import jax
import jax.numpy as jnp
from jax import lax
from jax.experimental import pallas as pl
from jax.experimental.pallas import tpu as pltpu
from jax.sharding import PartitionSpec as P

MESH = pl.DeviceIdType.MESH
HIGHEST = lax.Precision.HIGHEST
F32 = jnp.float32
BF16 = jnp.bfloat16
NX, NZL, NC, NY, NZH = 4, 4, 2, 4, 2
EPS = 1e-05


def coords():
    s = lax.axis_index("samples")
    v = lax.axis_index("variants")
    return s // 8, (s // 2) % 4, s % 2, v // 2, v % 2


def peer(dx=0, dzl=0, dc=0, dy=0, dzh=0):
    x, zl, c, y, zh = coords()
    x = (x + dx) % NX
    zl = (zl + dzl) % NZL
    c = (c + dc) % NC
    y = (y + dy) % NY
    zh = (zh + dzh) % NZH
    return ((x * NZL + zl) * NC + c, y * NZH + zh)


def loop(low, high, body):
    def step(k, carry):
        body(k)
        return carry

    lax.fori_loop(low, high, step, 0)


def iota(shape, axis):
    return lax.broadcasted_iota(jnp.int32, shape, axis)


NB = 64


def factor_diagonal(D, Y):
    big = (8, 128)
    n8 = NB // 8
    D = [D[8 * m : 8 * m + 8, :] for m in range(n8)]
    sub = iota(big, 0)
    for q in range(n8):
        rows = [jnp.broadcast_to(D[q][i : i + 1, :], big) for i in range(8)]
        lanes = [[jnp.broadcast_to(D[m][:, 8 * q + c : 8 * q + c + 1], big) for c in range(8)] for m in range(q, n8)]
        a = [[jnp.broadcast_to(lanes[0][c][i : i + 1, :], big) if c <= i else None for c in range(8)] for i in range(8)]
        r, l, y, z = [None] * 8, [[None] * 8 for _ in range(8)], [None] * 8, [None] * 8
        for i in range(8):
            r[i] = lax.rsqrt(a[i][i])
            for k in range(i + 1, 8):
                l[k][i] = a[k][i] * r[i]
            for k in range(i + 1, 8):
                for c in range(i + 1, k + 1):
                    a[k][c] = a[k][c] - l[k][i] * l[c][i]
            y[i] = rows[i] * r[i]
            for k in range(i + 1, 8):
                rows[k] = rows[k] - l[k][i] * y[i]
        out = y[0]
        for i in range(1, 8):
            out = jnp.where(sub == i, y[i], out)
        Y[8 * q : 8 * q + 8, :] = out
        for i in range(7, -1, -1):
            acc = y[i]
            for k in range(i + 1, 8):
                acc = acc - l[k][i] * z[k]
            z[i] = acc * r[i]
        for m in range(q + 1, n8):
            s = [lanes[m - q][k] * z[k] for k in range(8)]
            D[m] = D[m] - (((s[0] + s[1]) + (s[2] + s[3])) + ((s[4] + s[5]) + (s[6] + s[7])))


def factor_rows(M, Y, b):
    n = M.shape[0]
    at = slice(b * NB, (b + 1) * NB)
    eye = (iota((NB, NB), 0) == iota((NB, NB), 1)).astype(F32)
    factor_diagonal(jnp.concatenate([M[at, at], eye], axis=1), Y)
    first = b * NB // 128 * 128
    last = n + -(-(b + 1) * NB // 128) * 128
    panel = jnp.dot(Y[:, NB:], M[at, first:last], precision=HIGHEST, preferred_element_type=F32)
    M[at, first:last] = panel
    if (b + 1) * NB < n:
        rest = slice((b + 1) * NB, n)
        M[rest, first:last] = M[rest, first:last] - lax.dot_general(
            panel[:, (b + 1) * NB - first : n - first],
            panel,
            (((0,), (0,)), ((), ())),
            precision=HIGHEST,
            preferred_element_type=F32,
        )


def comm_kernel(
    count, x_hbm, sk_hbm, basis_ref, load_ref,
    X, skbuf, W, st, st_c, st_x, st_z, Pp, tr, di, mg, zsend, zrecv,
    PG, TT, trecv, TM, tx, TX, tz, tfin, gbuf, grecv, gxy, gz, gfin, M, Y, own_rows,
    x_sem, c_ssem, c_rsem, sk_ssem, sk_rsem, fw_ssem, fw_rsem, st_ssem, st_rsem, y_ssem, y_rsem,
    z_ssem, z_rsem, g_ssem, g_rsem, t_ssem, t_rsem, tc_ssem, tc_rsem,
):
    x, zl, c, y, zh = coords()
    v = y * NZH + zh
    vz = y * NZH + (1 - zh)
    xz = x * NZL + zl
    xy = x * NY + y
    z = zh * NZL + zl
    blocks, rows, cols = X.shape
    local_count = blocks * rows

    def load(i):
        return pltpu.make_async_copy(x_hbm.at[pl.ds(i * rows, rows)], X.at[i], x_sem.at[i])

    def send(src, dst, ssem, rsem, to):
        return pltpu.make_async_remote_copy(
            src_ref=src, dst_ref=dst, send_sem=ssem, recv_sem=rsem, device_id=to, device_id_type=MESH
        )

    load(0).start()
    barrier = pltpu.get_barrier_semaphore()

    def greet(to):
        pl.semaphore_signal(barrier, inc=1, device_id=to, device_id_type=MESH)

    loop(0, 4, lambda k: greet(peer(dzl=k, dzh=1)))
    loop(0, 9, lambda k: greet(peer(dx=k // 3 + 1, dy=k % 3 + 1)))
    sketch_in = pltpu.make_async_copy(sk_hbm, skbuf.at[xz, c], x_sem.at[blocks])
    sketch_in.start()
    loop(1, blocks, lambda i: load(i).start())
    loop(1, 4, lambda k: greet(peer(dzl=k)))
    loop(1, 4, lambda k: greet(peer(dx=k)))
    loop(1, 4, lambda k: greet(peer(dy=k)))
    greet(peer(dc=1))

    lane = 512
    order = (1, 3, 2)
    pieces = cols // lane

    load(0).wait()
    pivots = []
    for h in range(pieces):

        def add_rows(r, acc, h=h):
            d = X[0, pl.ds(pl.multiple_of(r * 16, 16), 16), pl.ds(h * lane, lane)].astype(F32)
            return acc + (d[:8] + d[8:])

        acc = lax.fori_loop(0, rows // 16, add_rows, jnp.zeros((8, lane), F32), unroll=4)
        pivots.append(jnp.sum(acc, axis=0, keepdims=True) / rows)

    def spread_of(i, carry):
        out = []
        for h in range(pieces):

            def add_rows(r, acc, h=h):
                s1, s2 = acc
                d = X[i, pl.ds(pl.multiple_of(r * 16, 16), 16), pl.ds(h * lane, lane)].astype(F32) - pivots[h]
                q = d * d
                return s1 + (d[:8] + d[8:]), s2 + (q[:8] + q[8:])

            out.append(lax.fori_loop(0, rows // 16, add_rows, carry[h], unroll=4))
        return tuple(out)

    zero = jnp.zeros((8, lane), F32)
    sums = tuple((zero, zero) for _ in range(pieces))
    def block_sums(i, carry):
        @pl.when(i > 0)
        def _():
            load(i).wait()

        return spread_of(i, carry)

    early = 3
    sums = lax.fori_loop(0, early, block_sums, sums)

    pl.semaphore_wait(barrier, 23)

    def sketch_x(k):
        return send(skbuf.at[xz, c], skbuf.at[xz, c], sk_ssem.at[k], sk_rsem.at[k], peer(dx=k))

    def sketch_z(k):
        return send(skbuf.at[xz, c], skbuf.at[xz, c], sk_ssem.at[4 + k], sk_rsem.at[4 + k], peer(dzl=k))

    def sketch_zx(j, k):
        at = x * NZL + (zl + NZL - j) % NZL
        i = 4 * j + 4 + k
        return send(skbuf.at[at, c], skbuf.at[at, c], sk_ssem.at[i], sk_rsem.at[i], peer(dx=k))

    def sketch_core(k):
        at = pl.ds(((x + k) % NX) * NZL, NZL)
        return send(skbuf.at[at, c], skbuf.at[at, c], fw_ssem.at[k], fw_rsem.at[k], peer(dc=1))

    sketch_in.wait()
    for k in order:
        sketch_z(k).start()
    for k in order:
        sketch_x(k).start()

    sums = lax.fori_loop(early, blocks, block_sums, sums)

    for h in range(pieces):
        s1 = jnp.sum(sums[h][0], axis=0, keepdims=True)
        s2 = jnp.sum(sums[h][1], axis=0, keepdims=True)
        mean = pivots[h] + s1 / local_count
        m2 = s2 - s1 * s1 / local_count
        for q in range(lane // 128):
            g = h * (lane // 128) + q
            st[g : g + 1, :] = mean[:, q * 128 : (q + 1) * 128]
            st[16 + g : 17 + g, :] = m2[:, q * 128 : (q + 1) * 128]

    copy = send(st, st_c, c_ssem.at[0], c_rsem.at[0], peer(dc=1))
    copy.start()
    copy.wait()
    a, b = st[...], st_c[...]
    n = float(local_count)
    delta = a[:16] - b[:16]
    st_x[x, :16] = 0.5 * (a[:16] + b[:16])
    st_x[x, 16:] = a[16:] + b[16:] + (0.5 * n) * delta * delta
    n = 2.0 * n

    def merge(ref, n):
        mean = 0.25 * ((ref[0, :16] + ref[1, :16]) + (ref[2, :16] + ref[3, :16]))
        m2 = (ref[0, 16:] + ref[1, 16:]) + (ref[2, 16:] + ref[3, 16:])
        for i in range(4):
            d = ref[i, :16] - mean
            m2 = m2 + n * (d * d)
        return mean, m2

    def stat_x(k):
        return send(st_x.at[x], st_x.at[x], st_ssem.at[k], st_rsem.at[k], peer(dx=k))

    def stat_z(k):
        return send(st_z.at[zl], st_z.at[zl], st_ssem.at[4 + k], st_rsem.at[4 + k], peer(dzl=k))

    for k in order:
        stat_x(k).start()
    for j in order:
        sketch_z(j).wait()
        for k in order:
            sketch_zx(j, k).start()
    sketch_core(0).start()

    for k in order:
        stat_x(k).wait()
    mean, m2 = merge(st_x, n)
    n = 4.0 * n
    st_z[zl, :16] = mean
    st_z[zl, 16:] = m2
    loop(1, 4, lambda k: stat_z(k).start())

    loop(1, 4, lambda k: stat_z(k).wait())
    mean, m2 = merge(st_z, n)
    inv_sd = lax.rsqrt(m2 / count + EPS)
    st[:16, :] = mean
    st[16:, :] = inv_sd
    columns = jnp.transpose(jnp.concatenate([mean, inv_sd, jnp.zeros((96, 128), F32)], axis=0))

    for k in order:
        sketch_x(k).wait()
        for j in order:
            sketch_zx(j, k).wait()
        sketch_core(4 - k).start()
    for k in range(NX):
        sketch_core(k).wait()

    shift = jnp.zeros((8, 256), F32)
    for g in range(16):
        sk = skbuf[g].reshape(128, 256).astype(F32)
        w = (columns[:, 16 + g : 17 + g] * sk).astype(BF16)
        W[g * 128 : (g + 1) * 128, :] = w
        shift = shift + jnp.sum((columns[:, g : g + 1] * w.astype(F32)).reshape(16, 8, 256), axis=0)
    shift = jnp.sum(shift, axis=0, keepdims=True)

    def project(i):
        Pp[i] = jnp.dot(X[i], W[...], preferred_element_type=F32) - shift

    size = rows // 2
    half = size // 2

    def block(dy, p):
        return ((y + dy) % NY) * NZH + (1 - zh if p < 2 else zh)

    def part(dy, p, h):
        return Pp.at[block(dy, p), pl.ds(p % 2 * size + h * half, half)]

    def transit(p, h):
        i = 6 * p + h
        return send(part(2, p, h), tr.at[p, h], y_ssem.at[i], y_rsem.at[i], peer(dy=1 if h == 0 else 3))

    def direct(p, h):
        i = 6 * p + 2 + h
        dy = 3 if h == 0 else 1
        return send(part(dy, p, h), di.at[p, h], y_ssem.at[i], y_rsem.at[i], peer(dy=dy))

    def merged(p, h):
        i = 6 * p + 4 + h
        dy = 1 if h == 0 else 3
        return send(part(dy, p, h), mg.at[p, h], y_ssem.at[i], y_rsem.at[i], peer(dy=dy))

    def start(copy, p):
        copy(p, 0).start()
        copy(p, 1).start()

    def pass_on(p):
        for h in range(2):
            transit(p, h).wait()
            at = pl.ds(p % 2 * size + h * half, half)
            i = block(1 if h == 0 else 3, p)
            Pp[i, at] = Pp[i, at] + tr[p, h]
            merged(p, h).start()

    def arrived(p):
        for h in range(2):
            direct(p, h).wait()
            merged(p, h).wait()
        return Pp[block(0, p), pl.ds(p % 2 * size, size)] + (di[p] + mg[p]).reshape(size, -1)

    def z_copy(p):
        return send(zsend.at[p], zrecv.at[p], z_ssem.at[p], z_rsem.at[p], peer(dzh=1))

    project(block(2, 0))
    start(transit, 0)
    start(transit, 1)
    loop(0, 2, lambda q: project(block(1 + 2 * q, 0)))
    start(direct, 0)
    start(direct, 1)
    loop(0, 5, lambda q: project(((y + q) % NY) * NZH + zh + (4 - q) // 4 * (1 - 2 * zh)))
    pass_on(0)
    pass_on(1)
    zsend[0] = arrived(0)
    z_copy(0).start()
    zsend[1] = arrived(1)
    z_copy(1).start()
    start(transit, 2)
    start(transit, 3)
    start(direct, 2)
    start(direct, 3)
    pass_on(2)
    pass_on(3)
    for p in range(2):
        here = arrived(2 + p)
        z_copy(p).wait()
        own_rows[p * size : (p + 1) * size] = here + zrecv[p]
    own = own_rows[...]

    PG[v] = jnp.transpose(own).astype(BF16)

    def gather_own(k):
        return send(PG.at[v], PG.at[v], y_ssem.at[24 + k], y_rsem.at[24 + k], peer(dy=k))

    def gather_other(k):
        return send(PG.at[vz], PG.at[vz], y_ssem.at[28 + k], y_rsem.at[28 + k], peer(dy=k))

    gather_z = send(PG.at[v], PG.at[v], z_ssem.at[2], z_rsem.at[2], peer(dzh=1))
    gather_z.start()

    gram = lax.dot_general(own, own, (((0,), (0,)), ((), ())), precision=HIGHEST, preferred_element_type=F32)
    gbuf[...] = (gram / count).reshape(gbuf.shape)
    g_core = send(gbuf.at[1 - c], grecv, c_ssem.at[2], c_rsem.at[2], peer(dc=1))
    g_core.start()
    g_core.wait()
    gbuf[c] = gbuf[c] + grecv[...]
    gxy[xy] = gbuf[c, xy]

    def gram_scatter(k):
        to = ((x + k // 4) % NX) * NY + (y + k % 4) % NY
        return send(gbuf.at[c, to], gxy.at[xy], g_ssem.at[k], g_rsem.at[k], peer(dx=k // 4, dy=k % 4))

    def gram_z(k):
        return send(gz.at[z], gz.at[z], g_ssem.at[16 + k], g_rsem.at[16 + k], peer(dzh=k // 4, dzl=k % 4))

    def gram_gather(k):
        return send(gfin.at[c, xy], gfin.at[c, xy], g_ssem.at[24 + k], g_rsem.at[24 + k], peer(dx=k // 4, dy=k % 4))

    loop(1, 16, lambda k: gram_scatter(k).start())
    for k in order:
        gather_own(k).start()
    gather_z.wait()
    for k in order:
        gather_other(k).start()
    loop(1, 16, lambda k: gram_scatter(k).wait())
    gz[z] = jnp.sum(gxy[...], axis=0)
    loop(1, 8, lambda k: gram_z(k).start())


    loop(1, 8, lambda k: gram_z(k).wait())
    gfin[c, xy] = jnp.sum(gz[...], axis=0)
    loop(1, 16, lambda k: gram_gather(k).start())

    loop(1, 4, lambda k: gather_own(k).wait())

    def products(j, which):
        at = pl.ds(pl.multiple_of(j * 256, 256), 256)
        acc = jnp.zeros((256, 256), F32)
        for i in which:
            acc = acc + jnp.dot(PG[i], X[i, :, at], preferred_element_type=F32)
        return acc.reshape(2, 128, 256)

    def first_product(j):
        TT[j] = products(j, [q * NZH + zh for q in range(NY)] + [vz])

    loop(0, 8, first_product)

    loop(1, 4, lambda k: gather_other(k).wait())
    total = jnp.zeros((256, 128), F32)
    for i in range(8):
        part = PG[i].astype(F32)
        total = total + (part[:, :128] + part[:, 128:])
    total = jnp.sum(total, axis=1, keepdims=True).reshape(2, 128, 1)
    root = math.sqrt(count)

    def t_core(j):
        return send(TT.at[j, 1 - c], trecv.at[j], tc_ssem.at[j], tc_rsem.at[j], peer(dc=1))

    def second_product(j):
        acc = TT[j] + products(j, [((y + k) % NY) * NZH + 1 - zh for k in order])
        mean = jnp.concatenate([st[pl.ds(2 * j, 1), :], st[pl.ds(2 * j + 1, 1), :]], axis=1)
        inv_sd = jnp.concatenate([st[pl.ds(16 + 2 * j, 1), :], st[pl.ds(17 + 2 * j, 1), :]], axis=1)
        TT[j] = (inv_sd / root) * (acc - total * mean)
        t_core(j).start()

    for k in order + (0,):
        first = ((x + k) % NX) * 2
        loop(0, 2, lambda q: second_product(first + q))

    def t_x(k, h):
        to = ((x + k) % NX) * 2
        at = pl.ds(h * 64, 64)
        i = 4 * h + k
        return send(TM.at[pl.ds(to, 2), at], tx.at[x, :, at], t_ssem.at[i], t_rsem.at[i], peer(dx=k))

    def t_z(k, h):
        i = 8 + 4 * h + k
        return send(TX.at[h, (zl + k) % NZL], tz.at[h, zl], t_ssem.at[i], t_rsem.at[i], peer(dzl=k))

    def merge_x(h):
        for k in order:
            t_x(k, h).wait()
        at = pl.ds(h * 64, 64)
        acc = TM[pl.ds(2 * x, 2), at]
        for k in order:
            acc = acc + tx[(x + k) % NX, :, at]
        for q in range(NZL):
            TX[h, q] = acc[q // 2, :, q % 2 * 128 : q % 2 * 128 + 128]
        for k in order:
            t_z(k, h).start()

    for k in order + (0,):
        for q in range(2):
            j = ((x + k) % NX) * 2 + q
            t_core(j).wait()
            TM[j] = TT[j, c] + trecv[j]
        if k:
            t_x(k, 0).start()
    for k in order:
        t_x(k, 1).start()

    loop(1, 16, lambda k: gram_gather(k).wait())
    g_back = send(gfin.at[c], gfin.at[c], c_ssem.at[3], c_rsem.at[3], peer(dc=1))
    g_back.start()
    g_back.wait()
    n = own.shape[1]
    M[:, :n] = gfin[...].reshape(n, n)
    M[:, n:] = (iota((n, n), 0) == iota((n, n), 1)).astype(F32)

    factor_rows(M, Y, 0)
    factor_rows(M, Y, 1)
    merge_x(0)
    factor_rows(M, Y, 2)
    merge_x(1)
    factor_rows(M, Y, 3)
    basis_ref[...] = lax.dot_general(
        own_rows[...], M[:, n:], (((1,), (1,)), ((), ())), precision=HIGHEST, preferred_element_type=F32
    )
    mine = pl.ds(pl.multiple_of(c * 128, 128), 128)
    for h in range(2):
        for k in order:
            t_z(k, h).wait()
        acc = TX[h, zl]
        for k in order:
            acc = acc + tz[h, (zl + k) % NZL]
        tfin[pl.ds(pl.multiple_of(c * 128 + h * 64, 64), 64)] = acc
    t_back = send(tfin.at[mine], tfin.at[mine], c_ssem.at[5], c_rsem.at[5], peer(dc=1))
    t_back.start()
    t_back.wait()
    loads = jnp.transpose(jnp.dot(M[:, n:], tfin[...], precision=HIGHEST, preferred_element_type=F32))
    load_ref[...] = jnp.where(c == 0, loads[:64], loads[64:])


def power_step(dosage, sketch, count):
    rows, cols = dosage.shape
    k = sketch.shape[1]
    vm = pltpu.VMEM
    dma = pltpu.SemaphoreType.DMA
    vmem = pl.BlockSpec(memory_space=pltpu.VMEM)
    return pl.pallas_call(
        functools.partial(comm_kernel, count),
        out_shape=(
            pltpu.VMEM((rows // 8, k), F32),
            pltpu.VMEM((64, k), F32),
        ),
        in_specs=[pl.BlockSpec(memory_space=pl.ANY), pl.BlockSpec(memory_space=pl.ANY)],
        out_specs=(vmem, vmem),
        scratch_shapes=[
            vm((8, rows // 8, cols), BF16),
            vm((16, 2, 64, k), BF16),
            vm((cols, k), BF16),
            vm((32, 128), F32),
            vm((32, 128), F32),
            vm((4, 32, 128), F32),
            vm((4, 32, 128), F32),
            vm((8, rows // 8, k), F32),
            vm((4, 2, rows // 32, k), F32),
            vm((4, 2, rows // 32, k), F32),
            vm((4, 2, rows // 32, k), F32),
            vm((2, rows // 16, k), F32),
            vm((2, rows // 16, k), F32),
            vm((8, k, rows // 8), BF16),
            vm((8, 2, k // 2, cols // 8), F32),
            vm((8, k // 2, cols // 8), F32),
            vm((8, k // 2, cols // 8), F32),
            vm((4, 2, k // 2, cols // 8), F32),
            vm((2, 4, k // 4, 128), F32),
            vm((2, 4, k // 4, 128), F32),
            vm((k, 128), F32),
            vm((2, 16, 8, k), F32),
            vm((16, 8, k), F32),
            vm((16, 8, k), F32),
            vm((8, 8, k), F32),
            vm((2, 16, 8, k), F32),
            vm((k, 2 * k), F32),
            vm((NB, 2 * NB), F32),
            vm((rows // 8, k), F32),
            dma((9,)),
            dma((6,)), dma((6,)),
            dma((20,)), dma((20,)),
            dma((4,)), dma((4,)),
            dma((8,)), dma((8,)),
            dma((32,)), dma((32,)),
            dma((3,)), dma((3,)),
            dma((40,)), dma((40,)),
            dma((16,)), dma((16,)),
            dma((8,)), dma((8,)),
        ],
        compiler_params=pltpu.CompilerParams(
            collective_id=0, has_side_effects=True, vmem_limit_bytes=56 * 2**20
        ),
        name="power_step",
    )(dosage, sketch)


def store_kernel(basis_ref, load_ref, basis_out, load_out, sem):
    copies = [
        pltpu.make_async_copy(basis_ref, basis_out, sem.at[0]),
        pltpu.make_async_copy(load_ref, load_out, sem.at[1]),
    ]
    for copy in copies:
        copy.start()
    for copy in copies:
        copy.wait()


def store(basis, loadings):
    vmem = pl.BlockSpec(memory_space=pltpu.VMEM)
    hbm = pl.BlockSpec(memory_space=pltpu.HBM)
    return pl.pallas_call(
        store_kernel,
        out_shape=(jax.ShapeDtypeStruct(basis.shape, F32), jax.ShapeDtypeStruct(loadings.shape, F32)),
        in_specs=[vmem, vmem],
        out_specs=(hbm, hbm),
        scratch_shapes=[pltpu.SemaphoreType.DMA((2,))],
        name="store",
    )(basis, loadings)


def local(dosage, sketch):
    count = dosage.shape[0] * lax.axis_size("samples")
    return store(*power_step(dosage, sketch, count))


def solution(mesh):
    in_specs = (P("samples", "variants"), P(("variants", "samples"), None))
    out_specs = (P(("samples", "variants"), None), P(("variants", "samples"), None))
    return jax.shard_map(local, mesh=mesh, in_specs=in_specs, out_specs=out_specs, check_vma=False)
```
